32 devices in a mesh: groups: 2 (over x), blk: 16 (over z, y, core).
Axes of the slice: x: 2, y: 2, z: 4, core: 2. Of those that a mesh axis runs over, the one named last changes fastest.
Arguments:
- queries: bfloat16 [12288, 3072], P(('groups', 'blk')), parts along dimension 0, may hold values from -4.5 to 4.5
- keys_values: bfloat16 [2, 12288, 3072], P(None, ('groups', 'blk')), parts along dimension 1, may hold values from -4.5 to 4.5
- key_blocks: int32 [96, 8], P(('groups', 'blk')), parts along dimension 0, may hold values from 0 to 47, as said below
- pair_count: int32 [96], P(('groups', 'blk')), parts along dimension 0, may hold values from 6 to 8
Outputs:
- attended: bfloat16 [12288, 3072], P(('groups', 'blk')), parts along dimension 0
The draws below stay inside these ranges and needn't reach their ends.
There are 2 independent parts, one for each index of `groups`. The reference program is written for one: setup_inputs(seed, part) draws one part's arguments, and reference() takes and returns one part's arrays. A program takes and returns all parts, laid end to end along the dimension named above; each array names one. Nothing has to cross between parts.
Inputs may be any that keep to these rules, and one draw needn't show every extreme that they name: `key_blocks`: row r holds 8 distinct blocks, all held by devices at most 2 places away from the device of block r along the closed cycle of devices (block b lies on device b // 3, devices 0 and the last are neighbours); the first entry is r itself. Entries at j >= pair_count[r] are not pairs.
All inputs are finite; a program needn't handle non-finite values.
Results may differ from the reference program's by a relative error of at most 0.0046.
Values may be sent and summed in bfloat16 or wider, within the bound.
A program may use at most 128 MiB of HBM per device.

```python
import jax
import jax.numpy as jnp
from jax import lax

H = 24
HD = 128
BLK = 128
REACH = 2
NB = 8
QB_DEV = 3
TOKENS = 6144
QBLOCKS = 48


def draw_queries(key, part):
    key = jax.random.fold_in(key, 11)
    normal_key = jax.random.fold_in(key, 0)
    initial = jnp.clip(jax.random.normal(normal_key, (TOKENS, H * HD)), -4.5, 4.5)
    return initial.astype(jnp.bfloat16)


def draw_keys_values(key, part):
    key = jax.random.fold_in(key, 12)
    normal_key = jax.random.fold_in(key, 0)
    initial = jnp.clip(jax.random.normal(normal_key, (2, TOKENS, H * HD)), -4.5, 4.5)
    return initial.astype(jnp.bfloat16)


def draw_key_blocks(key, part):
    key = jax.random.fold_in(key, 21)
    window_blocks = (2 * REACH + 1) * QB_DEV
    row_index = jnp.arange(QBLOCKS, dtype=jnp.int32)
    device_index = row_index // QB_DEV
    ranks = jax.random.randint(key, (QBLOCKS, window_blocks), 0, 2 ** 20)
    ranks = ranks * window_blocks + jnp.arange(window_blocks, dtype=jnp.int32)[None, :]
    own_slot = REACH * QB_DEV + row_index % QB_DEV
    ranks = jnp.where(jnp.arange(window_blocks, dtype=jnp.int32)[None, :] == own_slot[:, None], -1, ranks)
    ranked = jnp.argsort(ranks, axis=1)[:, :NB].astype(jnp.int32)
    block_ids = jnp.mod(device_index[:, None] * QB_DEV - REACH * QB_DEV + ranked, QBLOCKS)
    return block_ids.astype(jnp.int32)


def draw_pair_count(key, part):
    key = jax.random.fold_in(key, 22)
    counts = jax.random.randint(key, (QBLOCKS,), NB - 2, NB + 1)
    counts = counts.at[0].set(NB).at[1].set(NB - 2)
    return counts.astype(jnp.int32)


def setup_inputs(seed: int = 0, part: int = 0) -> dict:
    key_list = jax.random.split(jax.random.key(seed), 5)
    part_splits = jax.random.split(jax.random.fold_in(key_list[4], part), 5)
    return {
        "queries": draw_queries(jax.random.fold_in(jax.random.fold_in(key_list[4], part), 71), part),
        "keys_values": draw_keys_values(jax.random.fold_in(jax.random.fold_in(key_list[4], part), 71), part),
        "key_blocks": draw_key_blocks(jax.random.fold_in(jax.random.fold_in(key_list[4], part), 71), part),
        "pair_count": draw_pair_count(jax.random.fold_in(jax.random.fold_in(key_list[4], part), 71), part),
    }


def reference(queries, keys_values, key_blocks, pair_count):
    tokens, feature_width = queries.shape
    blocks = tokens // BLK
    query_blocks = queries.reshape(blocks, BLK, H, HD)
    keyval_blocks = keys_values.reshape(2, blocks, BLK, H, HD)
    scale_factor = HD ** -0.5

    def attend_block(args):
        qblock, block_ids, live_count = args
        selected = keyval_blocks[:, block_ids.astype(jnp.int32)]
        key_rows = selected[0].reshape(NB * BLK, H, HD).astype(jnp.float32)
        value_rows = selected[1].reshape(NB * BLK, H, HD).astype(jnp.float32)
        scores = jnp.einsum("qhd,khd->hqk", qblock.astype(jnp.float32), key_rows) * scale_factor
        live_mask = jnp.repeat(jnp.arange(NB) < live_count, BLK)
        scores = jnp.where(live_mask[None, None, :], scores, -1e30)
        row_max = jnp.max(scores, axis=-1, keepdims=True)
        weights = jnp.exp(scores - row_max)
        denominator = jnp.sum(weights, axis=-1)
        rounded = lax.optimization_barrier(weights.astype(jnp.bfloat16)).astype(jnp.float32)
        mixed = jnp.einsum("hqk,khd->qhd", rounded, value_rows)
        return (mixed / jnp.transpose(denominator)[:, :, None]).astype(jnp.bfloat16)

    result = lax.map(attend_block, (query_blocks, key_blocks, pair_count))
    return result.reshape(tokens, feature_width)
```

```python
import functools

import jax
import jax.numpy as jnp
from jax import lax
from jax.experimental import pallas as pl
from jax.experimental.pallas import tpu as pltpu
from jax.sharding import PartitionSpec as P

HD = 128
BLK = 128
NB = 8
AHEAD = 3
MESH = pl.DeviceIdType.MESH
FAR = -1e30
SCALE = HD ** (-0.5) * 1.4426950408889634


def kernel(n, q_hbm, kv_hbm, blocks_ref, count_ref, out_hbm,
           q_v, own_v, held, out_v, bias,
           in_sem, out_sem,
           y_send, c_send, z_send, p_send, recv):
    groups = held.shape[1]
    rows = q_v.shape[0]
    per_device = rows // BLK
    me = lax.axis_index("blk")
    core = me % 2
    side = (me // 2) % 2
    y_dev = me + 2 - 4 * side
    c_dev = me + 1 - 2 * core
    up = lax.rem(me + 4, n)
    down = lax.rem(me + n - 4, n)
    z_dev = jnp.where(side == 0, up, down)
    far_step = n - 2 + 4 * side
    passed_slot = (side + core) % 2
    other_passes_far = 1 - passed_slot
    far_dev = lax.rem(me + far_step, n)
    pass_dev = jnp.where(
        other_passes_far == 1,
        lax.rem(c_dev + far_step, n),
        c_dev + 2 - 4 * side,
    )
    sources = [me, y_dev, far_dev, c_dev, pass_dev]

    def columns(g):
        return pl.ds(pl.multiple_of(g * HD, HD), HD)

    def y_copy(g):
        return pltpu.make_async_remote_copy(
            src_ref=kv_hbm.at[:, :, columns(g)], dst_ref=held.at[0, g],
            send_sem=y_send.at[g], recv_sem=recv.at[0, g],
            device_id={"blk": y_dev}, device_id_type=MESH)

    def z_copy(g):
        return pltpu.make_async_remote_copy(
            src_ref=held.at[0, g], dst_ref=held.at[1, g],
            send_sem=z_send.at[g], recv_sem=recv.at[1, g],
            device_id={"blk": z_dev}, device_id_type=MESH)

    def c_copy(g):
        return pltpu.make_async_remote_copy(
            src_ref=kv_hbm.at[:, :, columns(g)], dst_ref=held.at[2, g],
            send_sem=c_send.at[g], recv_sem=recv.at[2, g],
            device_id={"blk": c_dev}, device_id_type=MESH)

    def p_copy(g):
        return pltpu.make_async_remote_copy(
            src_ref=held.at[passed_slot, g], dst_ref=held.at[3, g],
            send_sem=p_send.at[g], recv_sem=recv.at[3, g],
            device_id={"blk": c_dev}, device_id_type=MESH)

    def out_copy(g):
        return pltpu.make_async_copy(
            out_v.at[:, columns(g)], out_hbm.at[:, columns(g)], out_sem.at[g])

    q_in = pltpu.make_async_copy(q_hbm, q_v, in_sem.at[0])
    own_in = pltpu.make_async_copy(kv_hbm, own_v, in_sem.at[1])

    barrier = pltpu.get_barrier_semaphore()
    for dev in (y_dev, c_dev, up, down):
        pl.semaphore_signal(barrier, inc=1, device_id={"blk": dev}, device_id_type=MESH)
    pl.semaphore_wait(barrier, 4)

    for g in range(min(AHEAD, groups)):
        y_copy(g).start()
        c_copy(g).start()
    q_in.start()
    own_in.start()

    for r in range(per_device):
        for s, dev in enumerate(sources):
            for j in range(per_device):
                block = dev * per_device + j
                hit = jnp.int32(0)
                for i in range(NB):
                    listed = (blocks_ref[r, i] == block) & (i < count_ref[r])
                    hit = jnp.where(listed, 1, hit)
                value = jnp.where(hit == 1, 0.0, FAR).astype(jnp.float32)
                at = s * rows + j * BLK
                bias[r, :, at:at + BLK] = jnp.full((8, BLK), value, jnp.float32)
    q_in.wait()
    own_in.wait()

    def attend(g):
        q = q_v[:, columns(g)]
        keys = [own_v[0, :, columns(g)]] + [held[s, g, 0] for s in range(4)]
        values = [own_v[1, :, columns(g)]] + [held[s, g, 1] for s in range(4)]
        top = None
        scores = []
        for s in range(5):
            part = lax.dot_general(
                q, keys[s], (((1,), (1,)), ((), ())),
                preferred_element_type=jnp.float32)
            part = jnp.concatenate(
                [part[r * BLK:(r + 1) * BLK] + bias[r, 0:1, s * rows:(s + 1) * rows]
                 for r in range(per_device)], axis=0)
            best = jnp.max(part, axis=-1, keepdims=True)
            top = best if top is None else jnp.maximum(top, best)
            scores.append(part)
        total = None
        mixed = None
        for s in range(5):
            weights = jnp.exp2((scores[s] - top) * SCALE)
            added = jnp.sum(weights, axis=-1, keepdims=True)
            product = jnp.dot(
                weights.astype(jnp.bfloat16), values[s],
                preferred_element_type=jnp.float32)
            total = added if total is None else total + added
            mixed = product if mixed is None else mixed + product
        out_v[:, columns(g)] = (mixed / total).astype(out_v.dtype)

    def step(t, carry):
        @pl.when(t < groups)
        def _():
            y_copy(t).wait_recv()
            z_copy(t).start()
            y_copy(t).wait_send()
            c_copy(t).wait_send()

            @pl.when(t + AHEAD < groups)
            def _():
                y_copy(t + AHEAD).start()
                c_copy(t + AHEAD).start()

        @pl.when((t >= 1) & (t < groups + 1))
        def _():
            z_copy(t - 1).wait_recv()
            p_copy(t - 1).start()

        @pl.when(t >= 2)
        def _():
            g = t - 2
            c_copy(g).wait_recv()
            p_copy(g).wait_recv()
            attend(g)
            out_copy(g).start()

        return carry

    lax.fori_loop(0, groups + 2, step, 0)

    def finish(g, carry):
        z_copy(g).wait_send()
        p_copy(g).wait_send()
        out_copy(g).wait()
        return carry

    lax.fori_loop(0, groups, finish, 0)


def body(queries, keys_values, key_blocks, pair_count):
    rows, width = queries.shape
    groups = width // HD
    per_device = rows // BLK
    n = lax.axis_size("blk")
    any_spec = pl.BlockSpec(memory_space=pl.ANY)
    smem_spec = pl.BlockSpec(memory_space=pltpu.SMEM)
    dma = pltpu.SemaphoreType.DMA
    return pl.pallas_call(
        functools.partial(kernel, n),
        out_shape=jax.ShapeDtypeStruct((rows, width), jnp.bfloat16),
        in_specs=[any_spec, any_spec, smem_spec, smem_spec],
        out_specs=any_spec,
        scratch_shapes=[
            pltpu.VMEM((rows, width), jnp.bfloat16),
            pltpu.VMEM((2, rows, width), jnp.bfloat16),
            pltpu.VMEM((4, groups, 2, rows, HD), jnp.bfloat16),
            pltpu.VMEM((rows, width), jnp.bfloat16),
            pltpu.VMEM((per_device, 8, 5 * rows), jnp.float32),
            dma((2,)),
            dma((groups,)),
            dma((groups,)),
            dma((groups,)),
            dma((groups,)),
            dma((groups,)),
            dma((4, groups)),
        ],
        compiler_params=pltpu.CompilerParams(
            collective_id=0, has_side_effects=True,
            vmem_limit_bytes=56 * 1024 * 1024),
        cost_estimate=pl.CostEstimate(
            flops=4 * rows * 5 * rows * width,
            bytes_accessed=16 * rows * width,
            transcendentals=groups * rows * 5 * rows),
    )(queries, keys_values, key_blocks, pair_count)


def solution(mesh):
    placed = (
        P(("groups", "blk"), None),
        P(None, ("groups", "blk"), None),
        P(("groups", "blk"), None),
        P(("groups", "blk")),
    )
    return jax.shard_map(
        body, mesh=mesh, in_specs=placed, out_specs=P(("groups", "blk"), None), check_vma=False
    )
```

```python
import functools

import jax
import jax.numpy as jnp
from jax import lax
from jax.experimental import pallas as pl
from jax.experimental.pallas import tpu as pltpu
from jax.sharding import PartitionSpec as P

HD = 128
BLK = 128
NB = 8
SPLIT = 1
Z_LAG = 2
P_LAG = 1
AHEAD = 6
MESH = pl.DeviceIdType.MESH
FAR = -1e30
SCALE = HD ** (-0.5) * 1.4426950408889634


def kernel(n, q_hbm, kv_hbm, blocks_ref, count_ref, out_v,
           q_v, own_v, mate_v, held, bias, weights_v, total_v,
           in_sem, c_sem, y_send, z_send, p_send, recv):
    rows, width = q_v.shape
    groups = width // HD
    parts = 2 * SPLIT
    part_rows = rows // SPLIT
    pieces = groups * parts
    per_device = rows // BLK
    me = lax.axis_index("blk")
    core = me % 2
    side = (me // 2) % 2
    y_dev = me + 2 - 4 * side
    c_dev = me + 1 - 2 * core
    up = lax.rem(me + 4, n)
    down = lax.rem(me + n - 4, n)
    z_dev = jnp.where(side == 0, up, down)
    far_step = n - 2 + 4 * side
    passed_slot = (side + core) % 2
    other_passes_far = 1 - passed_slot
    far_dev = lax.rem(me + far_step, n)
    pass_dev = jnp.where(
        other_passes_far == 1,
        lax.rem(c_dev + far_step, n),
        c_dev + 2 - 4 * side,
    )
    sources = [me, y_dev, far_dev, pass_dev, c_dev]

    def columns(g):
        return pl.ds(pl.multiple_of(g * HD, HD), HD)

    def piece(p):
        g, k = p // parts, p % parts
        at = pl.multiple_of(k % SPLIT * part_rows, part_rows)
        return kv_hbm.at[k // SPLIT, pl.ds(at, part_rows), columns(g)]

    def landed(slot, p):
        g, k = p // parts, p % parts
        at = pl.multiple_of(k % SPLIT * part_rows, part_rows)
        return held.at[slot, g, k // SPLIT, pl.ds(at, part_rows)]

    def y_copy(g):
        return pltpu.make_async_remote_copy(
            src_ref=piece(g), dst_ref=landed(0, g),
            send_sem=y_send.at[g], recv_sem=recv.at[0, g],
            device_id={"blk": y_dev}, device_id_type=MESH)

    def z_copy(g):
        return pltpu.make_async_remote_copy(
            src_ref=landed(0, g), dst_ref=landed(1, g),
            send_sem=z_send.at[g], recv_sem=recv.at[1, g],
            device_id={"blk": z_dev}, device_id_type=MESH)

    c_copy = pltpu.make_async_remote_copy(
        src_ref=kv_hbm, dst_ref=mate_v,
        send_sem=c_sem.at[0], recv_sem=c_sem.at[1],
        device_id={"blk": c_dev}, device_id_type=MESH)

    def p_copy(g):
        return pltpu.make_async_remote_copy(
            src_ref=landed(passed_slot, g), dst_ref=landed(2, g),
            send_sem=p_send.at[g], recv_sem=recv.at[2, g],
            device_id={"blk": c_dev}, device_id_type=MESH)

    q_in = pltpu.make_async_copy(q_hbm, q_v, in_sem.at[0])
    own_in = pltpu.make_async_copy(kv_hbm, own_v, in_sem.at[1])

    barrier = pltpu.get_barrier_semaphore()
    for dev in (y_dev, c_dev, up, down):
        pl.semaphore_signal(barrier, inc=1, device_id={"blk": dev}, device_id_type=MESH)
    pl.semaphore_wait(barrier, 4)

    for g in range(min(AHEAD, pieces)):
        y_copy(g).start()
    q_in.start()
    own_in.start()
    c_copy.start()

    for r in range(per_device):
        for s, dev in enumerate(sources):
            for j in range(per_device):
                block = dev * per_device + j
                hit = jnp.int32(0)
                for i in range(NB):
                    listed = (blocks_ref[r, i] == block) & (i < count_ref[r])
                    hit = jnp.where(listed, 1, hit)
                value = jnp.where(hit == 1, 0.0, FAR).astype(jnp.float32)
                at = s * rows + j * BLK
                bias[r, :, at:at + BLK] = jnp.full((8, BLK), value, jnp.float32)
    q_in.wait()
    own_in.wait()

    def weigh(g):
        q = q_v[:, columns(g)]
        keys = [own_v[0, :, columns(g)]]
        keys += [held[s, g, 0] for s in range(3)]
        keys += [mate_v[0, :, columns(g)]]
        top = None
        scores = []
        for s in range(5):
            part = lax.dot_general(
                q, keys[s], (((1,), (1,)), ((), ())),
                preferred_element_type=jnp.float32)
            part = jnp.concatenate(
                [part[r * BLK:(r + 1) * BLK] + bias[r, 0:1, s * rows:(s + 1) * rows]
                 for r in range(per_device)], axis=0)
            best = jnp.max(part, axis=-1, keepdims=True)
            top = best if top is None else jnp.maximum(top, best)
            scores.append(part)
        total = None
        for s in range(5):
            weights = jnp.exp2((scores[s] - top) * SCALE)
            added = jnp.sum(weights, axis=-1, keepdims=True)
            total = added if total is None else total + added
            weights_v[s] = weights.astype(jnp.bfloat16)
        total_v[...] = jnp.broadcast_to(1.0 / total, total_v.shape)

    def mix(g):
        values = [own_v[1, :, columns(g)]]
        values += [held[s, g, 1] for s in range(3)]
        values += [mate_v[1, :, columns(g)]]
        mixed = None
        for s in range(5):
            product = jnp.dot(
                weights_v[s], values[s], preferred_element_type=jnp.float32)
            mixed = product if mixed is None else mixed + product
        out_v[:, columns(g)] = (mixed * total_v[...]).astype(out_v.dtype)

    def step(t, carry):
        @pl.when(t < pieces)
        def _():
            y_copy(t).wait_recv()
            z_copy(t).start()
            y_copy(t).wait_send()

            @pl.when(t + AHEAD < pieces)
            def _():
                y_copy(t + AHEAD).start()

        @pl.when((t >= Z_LAG) & (t < pieces + Z_LAG))
        def _():
            z_copy(t - Z_LAG).wait_recv()
            p_copy(t - Z_LAG).start()

        done = t - Z_LAG - P_LAG

        @pl.when(done == 0)
        def _():
            c_copy.wait_recv()

        @pl.when(done >= 0)
        def _():
            p_copy(done).wait_recv()

        @pl.when((done >= 0) & (done % parts == SPLIT - 1))
        def _():
            weigh(done // parts)

        @pl.when((done >= 0) & (done % parts == parts - 1))
        def _():
            mix(done // parts)

        return carry

    lax.fori_loop(0, pieces + Z_LAG + P_LAG, step, 0)

    def finish(p, carry):
        z_copy(p).wait_send()
        p_copy(p).wait_send()
        return carry

    lax.fori_loop(0, pieces, finish, 0)
    c_copy.wait_send()


def body(queries, keys_values, key_blocks, pair_count):
    rows, width = queries.shape
    groups = width // HD
    pieces = 2 * SPLIT * groups
    per_device = rows // BLK
    n = lax.axis_size("blk")
    any_spec = pl.BlockSpec(memory_space=pl.ANY)
    smem_spec = pl.BlockSpec(memory_space=pltpu.SMEM)
    dma = pltpu.SemaphoreType.DMA
    return pl.pallas_call(
        functools.partial(kernel, n),
        out_shape=pltpu.VMEM((rows, width), jnp.bfloat16),
        in_specs=[any_spec, any_spec, smem_spec, smem_spec],
        out_specs=pl.BlockSpec(memory_space=pltpu.VMEM),
        scratch_shapes=[
            pltpu.VMEM((rows, width), jnp.bfloat16),
            pltpu.VMEM((2, rows, width), jnp.bfloat16),
            pltpu.VMEM((2, rows, width), jnp.bfloat16),
            pltpu.VMEM((3, groups, 2, rows, HD), jnp.bfloat16),
            pltpu.VMEM((per_device, 8, 5 * rows), jnp.float32),
            pltpu.VMEM((5, rows, rows), jnp.bfloat16),
            pltpu.VMEM((rows, HD), jnp.float32),
            dma((2,)),
            dma((2,)),
            dma((pieces,)),
            dma((pieces,)),
            dma((pieces,)),
            dma((3, pieces)),
        ],
        compiler_params=pltpu.CompilerParams(
            collective_id=0, has_side_effects=True,
            vmem_limit_bytes=56 * 1024 * 1024),
        cost_estimate=pl.CostEstimate(
            flops=4 * rows * 5 * rows * width,
            bytes_accessed=16 * rows * width,
            transcendentals=groups * rows * 5 * rows),
    )(queries, keys_values, key_blocks, pair_count)


def solution(mesh):
    placed = (
        P(("groups", "blk"), None),
        P(None, ("groups", "blk"), None),
        P(("groups", "blk"), None),
        P(("groups", "blk")),
    )
    return jax.shard_map(
        body, mesh=mesh, in_specs=placed, out_specs=P(("groups", "blk"), None), check_vma=False
    )
```
